128 devices in a mesh: ox: 16 (over y, x), oy: 8 (over z, core).
Axes of the slice: x: 4, y: 4, z: 4, core: 2. Of those that a mesh axis runs over, the one named last changes fastest.
Arguments:
- atm_flux: float32 [4096, 6, 128], P(('ox', 'oy')), may hold values from -6 to 6
- pair_weight: float32 [12288, 128, 256], P(('ox', 'oy')), may hold values from -0.5 to 0.5
- pair_src: int32 [12288], P(('ox', 'oy')), may hold values from 0 to 31
- pair_dest: int32 [12288, 1], P(('ox', 'oy')), may hold values from 0 to 127; in each aligned block of 96 rows (0 to 95, 96 to 191, ...) at most 2 rows name the same one
- pair_block: int32 [12288], P(('ox', 'oy')), may hold values from 0 to 15
- ocean_state: float32 [80, 6, 256, 2048], P(None, None, 'ox', 'oy'), may hold values from -6 to 6
- land_mask: int32 [256, 2048], P('ox', 'oy'), may hold values 0 or 1
- kpp_depth: int32 [256, 2048], P('ox', 'oy'), may hold values from 1 to 79
- mixing_scale: float32 [256, 2048], P('ox', 'oy'), may hold values from 0.2 to 5
Outputs:
- ocean_out: float32 [80, 6, 256, 2048], P(None, None, 'ox', 'oy')
- atm_surface: float32 [4096, 6, 128], P(('ox', 'oy'))
The draws below stay inside these ranges and needn't reach their ends.
Inputs may be any that keep to these rules, and one draw needn't show every extreme that they name: `pair_dest`: among the pairs of one device no ocean device is named more than 2 times, and in every draw some device names one ocean device exactly 2 times.
All inputs are finite; a program needn't handle non-finite values. No bound on the sum of `land_mask` on one device may be relied on, other than what follows from the above.
Results may differ from the reference program's by a relative error of at most 0.000094.
Values sent between devices are 32-bit elements; how exact they have to be, the bound alone decides.
A program may use at most 192 MiB of HBM per device.

```python
import math
import jax
import jax.numpy as jnp
import numpy as np
from jax import lax

FIELDS = 6
LEVELS = 80
TILE_X = 16
TILE_Y = 256
ATM_CELLS = 128
ATM_DEV = 32
PAIR_DEV = 96
SLOTS = 2
NX = 256
NY = 2048
ATM_BLOCKS = 4096
PAIRS = 12288
N_OX = 16
N_OY = 8


def place_ends(result, key, low, high):
    index_at = [jax.random.randint(jax.random.fold_in(key, axis), (), 0, length) for axis, length in enumerate(result.shape)]
    main_axis = result.shape.index(max(result.shape))
    next_to = index_at[:main_axis] + [(index_at[main_axis] + 1) % result.shape[main_axis]] + index_at[main_axis + 1:]
    return result.at[tuple(index_at)].set(low).at[tuple(next_to)].set(high)


def level_of(rng, extent, split, smallest, high):
    loudness = 1.0
    for axis_at, shards_of in split:
        steps = jax.random.uniform(jax.random.fold_in(jax.random.fold_in(rng, 6), axis_at), (shards_of,), jnp.float32, smallest / len(split), high / len(split))
        loudness = loudness * jnp.repeat(jnp.exp(steps), extent[axis_at] // shards_of).reshape((-1,) + (1,) * (len(extent) - 1 - axis_at))
    return loudness


def routed_block(key, own, number, rows, amount, top, reach, skew):
    ranking = jax.random.permutation(key, amount)
    packed, common = shares(amount, rows * top, reach, skew, True), shares(amount, rows * top, reach, skew, False)
    places = jnp.arange(amount)

    def named(sizes, turn):
        used = int((sizes > 0).sum())
        fixed = max(1, used // 4)
        passed = fixed + (places - fixed + turn * (used - fixed)) % max(1, amount - fixed)
        return jnp.zeros((amount,), jnp.int32).at[ranking[jnp.where(places < fixed, places, passed)]].set(jnp.asarray(sizes, jnp.int32))

    sizes = jnp.where(number % 4 == 0, named(packed, number // 4), named(common, number - number // 4 - 1))
    mixed = jax.random.permutation(jax.random.fold_in(own, 3), amount)
    giver, sink = mixed[0:amount // 2 * 2:2], mixed[1:amount // 2 * 2:2]
    room = jnp.minimum(sizes[giver] - 1, reach - sizes[sink]) // 2
    room = jnp.where((giver == ranking[0]) | (sink == ranking[0]) | (sizes[sink] == 0), 0, jnp.maximum(room, 0))
    passed = jax.random.randint(jax.random.fold_in(own, 4), (amount // 2,), 0, 1 << 20) % (room + 1)
    sizes = sizes.at[giver].add(-passed).at[sink].add(passed)
    labels = jnp.searchsorted(jnp.cumsum(sizes), jnp.arange(rows * top), side="right").astype(jnp.int32)
    table = labels.reshape(top, rows).T
    table = table[jax.random.permutation(jax.random.fold_in(own, 1), rows)]
    turn = jax.random.randint(jax.random.fold_in(own, 2), (rows, 1), 0, top)
    return jnp.take_along_axis(table, (jnp.arange(top)[None, :] + turn) % top, axis=1)


def shares(amount, total, limit, skew, full):
    portions = [(1 << 20) // math.isqrt(rank ** skew) + 1 for rank in range(1, amount + 1)]
    largest = limit if full else min(limit, max(-(-total // amount), total * portions[0] // sum(portions)))
    least = 1 if total - largest >= amount - 1 else 0
    counts, surplus = [largest] + [least] * (amount - 1), total - largest - least * (amount - 1)
    while surplus > 0:
        movable = [i for i in range(1, amount) if counts[i] < largest] or [i for i in range(1, amount) if counts[i] < limit]
        mass, remaining = sum([portions[i] for i in movable]), surplus
        for i in movable:
            addition = min(limit - counts[i], max(1, remaining * portions[i] // mass), surplus)
            counts[i] = counts[i] + addition
            surplus = surplus - addition
    return np.array(counts)


def noise(key, extent, spread, reach, cuts=(), kind=jnp.bfloat16):
    array = spread * jax.random.normal(key, extent, jnp.float32)
    if cuts:
        array = array * level_of(key, extent, cuts, -0.22, 0.18)
    return jnp.clip(array, -reach, reach).astype(kind)


def setup_inputs(seed: int = 0) -> dict:
    splits = jax.random.split(jax.random.key(seed), 10)
    atm_flux = noise(splits[0], (ATM_BLOCKS, FIELDS, ATM_CELLS), 1.0, 6.0, ((0, 128),), jnp.float32)
    pair_weight = noise(splits[1], (PAIRS, ATM_CELLS, TILE_Y), ATM_CELLS ** -0.5, 0.5, ((0, 128),), jnp.float32)
    pair_src = place_ends(jax.random.randint(splits[2], (PAIRS,), 0, ATM_DEV), jax.random.fold_in(splits[2], 1), 0, ATM_DEV - 1).astype(jnp.int32)
    pair_dest_keys = jax.random.split(jax.random.fold_in(splits[3], 1), PAIRS // PAIR_DEV)
    pair_dest_turns = jax.random.permutation(jax.random.fold_in(splits[3], 3), PAIRS // PAIR_DEV)
    pair_dest = jax.vmap(lambda own, number: routed_block(jax.random.fold_in(splits[3], 2), own, number, PAIR_DEV, N_OX * N_OY, 1, SLOTS, 2))(pair_dest_keys, pair_dest_turns).reshape((PAIRS, 1))
    pair_block = place_ends(jax.random.randint(splits[4], (PAIRS,), 0, TILE_X), jax.random.fold_in(splits[4], 1), 0, TILE_X - 1).astype(jnp.int32)
    ocean_state = noise(splits[5], (LEVELS, FIELDS, NX, NY), 1.0, 6.0, ((2, 16), (3, 8)), jnp.float32)
    land_mask = place_ends((jax.random.randint(splits[6], (NX, NY), 0, 5) < 4).astype(jnp.int32), jax.random.fold_in(splits[6], 1), 0, 1)
    kpp_depth = place_ends(jax.random.randint(splits[7], (NX, NY), 1, LEVELS), jax.random.fold_in(splits[7], 1), 1, LEVELS - 1).astype(jnp.int32)
    mixing_scale = jnp.clip(jnp.exp(math.log(5.0) - 3.218876 * jax.random.uniform(splits[8], (NX, NY), jnp.float32) ** level_of(splits[8], (NX, NY), ((0, 16), (1, 8)), -0.2, 0.2)), 0.2, 5.0)
    return {"atm_flux": atm_flux, "pair_weight": pair_weight, "pair_src": pair_src, "pair_dest": pair_dest, "pair_block": pair_block, "ocean_state": ocean_state, "land_mask": land_mask, "kpp_depth": kpp_depth, "mixing_scale": mixing_scale}


HIGHEST = lax.Precision.HIGHEST
VISCOSITY = 0.025
FORCING = 0.5
BACKGROUND = 0.05


def laplace(padded):
    return (padded[..., 2:, 1:-1] + padded[..., :-2, 1:-1] + padded[..., 1:-1, 2:]
            + padded[..., 1:-1, :-2] - 4.0 * padded[..., 1:-1, 1:-1])


def pad_zero(values):
    widths = [(0, 0)] * (values.ndim - 2) + [(1, 1), (1, 1)]
    return jnp.pad(values, widths)


def couplings(kpp_depth, mixing_scale, level_count):
    level_index = jnp.arange(level_count - 1, dtype=jnp.int32)[:, None, None]
    level_float = level_index.astype(jnp.float32)
    depth_float = kpp_depth.astype(jnp.float32)[None]
    sigma = (level_float + 1.0) / depth_float
    profile = BACKGROUND + 6.75 * sigma * (1.0 - sigma) * (1.0 - sigma)
    inside = level_index < kpp_depth[None]
    return mixing_scale[None] * jnp.where(inside, profile, BACKGROUND)


def thomas(coupling, right_side):
    zero_layer = jnp.zeros_like(coupling[:1])
    padded = jnp.concatenate([zero_layer, coupling, zero_layer], axis=0)
    lower_band = -padded[:-1]
    upper_band = -padded[1:]
    diagonal = 1.0 + padded[:-1] + padded[1:]

    def forward(carried, inputs):
        ratio_prev, value_prev = carried
        lower_now, upper_now, diagonal_now, right_now = inputs
        denominator = diagonal_now - lower_now * ratio_prev
        ratio_now = upper_now / denominator
        value_now = (right_now - lower_now * value_prev) / denominator
        return (ratio_now, value_now), (ratio_now, value_now)

    start = (jnp.zeros_like(coupling[0]), jnp.zeros_like(right_side[0]))
    ignored, (ratios, values) = lax.scan(forward, start, (lower_band, upper_band, diagonal, right_side))

    def backward(carried, inputs):
        ratio_now, value_now = inputs
        solved_now = value_now - ratio_now * carried
        return solved_now, solved_now

    ignored, solved = lax.scan(backward, jnp.zeros_like(right_side[0]), (ratios, values), reverse=True)
    return solved


def reference(atm_flux, pair_weight, pair_src, pair_dest, pair_block, ocean_state, land_mask, kpp_depth, mixing_scale):
    pair_total = pair_weight.shape[0]
    owner_dev = jnp.arange(pair_total, dtype=jnp.int32) // PAIR_DEV
    source_block = owner_dev * ATM_DEV + pair_src
    destination = pair_dest[:, 0]
    target_row = (destination // N_OY) * TILE_X + pair_block
    target_band = destination % N_OY
    gathered = atm_flux[source_block]
    contribution = jnp.einsum("gfa,gao->gfo", gathered, pair_weight, precision=HIGHEST)
    flux_grid = jnp.zeros((FIELDS, N_OX * TILE_X, N_OY, TILE_Y), jnp.float32)
    flux_grid = flux_grid.at[:, target_row, target_band, :].add(jnp.transpose(contribution, (1, 0, 2)))
    flux_grid = flux_grid.reshape(FIELDS, N_OX * TILE_X, N_OY * TILE_Y)
    wet_cells = land_mask.astype(jnp.float32)
    coupling = couplings(kpp_depth, mixing_scale, LEVELS)

    def per_field(inputs):
        field_now, forcing_now = inputs
        masked = wet_cells * field_now
        right_side = masked.at[0].add(FORCING * wet_cells * forcing_now)
        mixed_state = thomas(coupling, right_side)
        first_pass = wet_cells * laplace(pad_zero(masked))
        second_pass = wet_cells * laplace(pad_zero(first_pass))
        return mixed_state - VISCOSITY * second_pass

    updated = lax.map(per_field, (jnp.moveaxis(ocean_state, 1, 0), flux_grid))
    ocean_out = jnp.moveaxis(updated, 0, 1)
    surface_top = ocean_out[0].reshape(FIELDS, N_OX * TILE_X, N_OY, TILE_Y)
    returned = jnp.transpose(surface_top[:, target_row, target_band, :], (1, 0, 2))
    atm_terms = jnp.einsum("gfo,gao->gfa", returned, pair_weight, precision=HIGHEST)
    atm_surface = jnp.zeros((ATM_DEV * N_OX * N_OY, FIELDS, ATM_CELLS), jnp.float32).at[source_block].add(atm_terms)
    return ocean_out, atm_surface
```

```python
import functools

import jax
import jax.numpy as jnp
from jax import lax
from jax.experimental import pallas as pl
from jax.experimental.pallas import tpu as pltpu
from jax.sharding import PartitionSpec as P

MESH = pl.DeviceIdType.MESH
F32 = jnp.float32
BF16 = jnp.bfloat16
VISCOSITY = 0.025
FORCING = 0.5
BACKGROUND = 0.05

DEVICES = 128
FIELDS = 6
LEVELS = 80
SLABS = LEVELS * FIELDS
ROWS = 16
COLS = 256
PAIRS = 96
BLOCKS = 32
STRIPS = 24
PITCH = 32
SENT = 25
GROUP = 64
GROUPS = 8
CHUNKS = 5
CHUNK_LEVELS = LEVELS // CHUNKS
CHUNK = SLABS // CHUNKS


def split2(v):
    hi = v.astype(BF16)
    lo = (v - hi.astype(F32)).astype(BF16)
    return hi, lo


def iota(shape, dim):
    return lax.broadcasted_iota(jnp.int32, shape, dim)


def column_square(dest_ref):
    column = jnp.concatenate([dest_ref[...], jnp.full((128 - PAIRS, 1), -1, jnp.int32)], axis=0)
    down = jnp.broadcast_to(column.astype(F32), (128, 128))
    return down, down.T


FLUX_STEP = 8


def flux_kernel(src_ref, weight_ref, flux_ref, dest_ref, block_ref, out_ref, parts, contrib):
    step = pl.program_id(0)

    @pl.when(step == 0)
    def _():
        contrib[...] = jnp.zeros_like(contrib)

        def prepare(b, carry):
            rows = jnp.concatenate([flux_ref[b], jnp.zeros((2, 128), F32)], axis=0)
            hi = rows.astype(BF16).astype(F32)
            both = jnp.concatenate([hi, rows - hi], axis=0).astype(BF16)
            parts[b] = jnp.concatenate([both, both], axis=1)
            return carry

        lax.fori_loop(0, BLOCKS, prepare, 0)

    for i in range(FLUX_STEP):
        g = step * FLUX_STEP + i
        left = parts[src_ref[g]]
        hi, lo = split2(weight_ref[i])
        right = jnp.concatenate([hi, lo], axis=0)
        both = jnp.dot(left, right, preferred_element_type=F32)
        value = both[:8] + both[8:]
        at = pl.multiple_of(g * 8, 8)
        contrib[pl.ds(at, 8), :] = value[:, :128]
        contrib[pl.ds(pl.multiple_of(1024 + g * 8, 8), 8), :] = value[:, 128:]

    @pl.when(step == pl.num_programs(0) - 1)
    def _():
        down, across = column_square(dest_ref)
        same = (down == across) & (iota((128, 128), 0) < iota((128, 128), 1))
        rank = jnp.sum(same.astype(F32), axis=0, keepdims=True)
        dest_here = across == iota((128, 128), 0).astype(F32)
        places = [dest_here & (rank == float(j)) for j in range(2)]
        rows = jnp.concatenate([block_ref[...].astype(F32), jnp.zeros((1, 128 - PAIRS), F32)], axis=1) + 1.0
        ids = [jnp.sum(jnp.where(p, rows, 0.0), axis=1, keepdims=True) - 1.0 for p in places]
        lane = iota((128, 128), 1)
        out_ref[pl.ds(STRIPS, 128, stride=PITCH), :] = jnp.where(lane == 0, ids[0], ids[1])
        place = jnp.concatenate([p.astype(F32).astype(BF16) for p in places], axis=0)
        place = jnp.concatenate([place, place], axis=1)
        for f in range(FIELDS):
            for h in range(2):
                hi, lo = split2(contrib[pl.ds(h * 1024 + f, 128, stride=8), :])
                got = jnp.dot(place, jnp.concatenate([hi, lo], axis=0), preferred_element_type=F32)
                for j in range(2):
                    out_ref[pl.ds(j * 12 + 2 * f + h, 128, stride=PITCH), :] = got[j * 128:(j + 1) * 128]


def flux_call(pair_weight, atm_flux, pair_src, pair_dest, pair_block):
    whole = lambda shape: pl.BlockSpec(shape, lambda i, s: (0,) * len(shape))
    return pl.pallas_call(
        flux_kernel,
        out_shape=jax.ShapeDtypeStruct((DEVICES * PITCH, 128), F32),
        grid_spec=pltpu.PrefetchScalarGridSpec(
            num_scalar_prefetch=1,
            grid=(PAIRS // FLUX_STEP,),
            in_specs=[
                pl.BlockSpec((FLUX_STEP, 128, COLS), lambda i, s: (i, 0, 0)),
                whole((BLOCKS, FIELDS, 128)),
                whole((PAIRS, 1)),
                whole((1, PAIRS)),
            ],
            out_specs=whole((DEVICES * PITCH, 128)),
            scratch_shapes=[
                pltpu.VMEM((BLOCKS, 16, 256), BF16),
                pltpu.VMEM((2048, 128), F32),
            ],
        ),
        compiler_params=pltpu.CompilerParams(vmem_limit_bytes=32 << 20),
        name="contributions",
    )(pair_src, pair_weight, atm_flux, pair_dest, pair_block.reshape(1, PAIRS))


def laplace(v):
    height, width = v.shape
    return (
        (pltpu.roll(v, height - 1, 0) + pltpu.roll(v, 1, 0))
        + (pltpu.roll(v, width - 1, 1) + pltpu.roll(v, 1, 1))
        - 4.0 * v
    )


def pack_columns(state, mask_ref, packed):
    lane = iota((ROWS, 128), 1)

    def group(g, carry):
        def one(j, acc):
            first, last = acc
            slab = jnp.minimum(g * GROUP + j, SLABS - 1)
            shift = 2 * j
            here = (lane == shift) | (lane == shift + 1)
            low = pltpu.roll(state[slab, :, :128], shift, 1)
            high = pltpu.roll(state[slab, :, 128:], lax.rem(shift + 2, 128), 1)
            return jnp.where(here, low, first), jnp.where(here, high, last)

        zero = jnp.zeros((ROWS, 128), F32)
        first, last = lax.fori_loop(0, GROUP, one, (zero, zero), unroll=4)
        packed[0, g] = first
        packed[1, g] = last
        return carry

    lax.fori_loop(0, GROUPS, group, 0)
    wet = mask_ref[...].astype(F32)
    g, shift = SLABS // GROUP, 2 * (SLABS % GROUP)
    here = (lane == shift) | (lane == shift + 1)
    packed[0, g] = jnp.where(here, pltpu.roll(wet[:, :128], shift, 1), packed[0, g])
    packed[1, g] = jnp.where(here, pltpu.roll(wet[:, 128:], shift + 2, 1), packed[1, g])


def side_columns(rim, slab):
    g = slab // GROUP
    shift = 2 * (slab - g * GROUP)
    right = pltpu.roll(rim[0, g], lax.rem(128 - shift, 128), 1)
    left = pltpu.roll(rim[1, g], 126 - shift, 1)
    return jnp.where(iota((24, 128), 1) < 64, right, left)


def coupling_at(k, depth, scale):
    kf = k.astype(F32)
    sigma = (kf + 1.0) / depth
    rest = 1.0 - sigma
    profile = BACKGROUND + 6.75 * sigma * rest * rest
    value = scale * jnp.where(kf < depth, profile, BACKGROUND)
    return jnp.where(k >= 0, value, 0.0)


def sweep_up(state, mask_ref, depth_ref, scale_ref, value, ratio, first_inverse):
    for half in range(2):
        rows = pl.ds(8 * half, 8)
        wet = mask_ref[rows, :].astype(F32)
        depth = depth_ref[rows, :].astype(F32)
        scale = scale_ref[rows, :]

        def level(i, carry):
            below, open_now, values = carry
            k = LEVELS - 1 - i
            above = coupling_at(k - 1, depth, scale)
            inverse = 1.0 / (1.0 + above + below * open_now)
            ratio_now = above * inverse
            ratio[k, rows, :] = ratio_now
            weight = below * inverse
            wet_inverse = wet * inverse
            new = []
            for f in range(FIELDS):
                now = wet_inverse * state[k * FIELDS + f, rows, :] + weight * values[f]
                value[k * FIELDS + f, rows, :] = now
                new.append(now)

            @pl.when(k == 0)
            def _():
                first_inverse[rows, :] = inverse

            return above, 1.0 - ratio_now, tuple(new)

        zero = jnp.zeros((8, COLS), F32)
        lax.fori_loop(0, LEVELS, level, (zero, zero, (zero,) * FIELDS))


def ocean_level(k, state, rims, rim, wet_wide, value, ratio, response, previous):
    ratio_now = ratio[k]
    response[k] = jnp.where(k == 0, response[k], ratio_now * response[jnp.maximum(k - 1, 0)])
    for f in range(FIELDS):
        slab = k * FIELDS + f
        tall = jnp.concatenate([state[slab], rims[slab]], axis=0)
        wide = jnp.concatenate([tall, side_columns(rim, slab)], axis=1)
        first = wet_wide[...] * laplace(wet_wide[...] * wide)
        second = wet_wide[:ROWS, :COLS] * laplace(first)[:ROWS, :COLS]
        mixed = value[slab] + ratio_now * previous[f]
        previous[f] = mixed
        value[slab] = mixed - VISCOSITY * second


def exchange_kernel(
    out_hbm, state_hbm, mask_ref, depth_ref, scale_ref,
    base_hbm, response, forced, answered,
    state, value, ratio, rims, mask_rims, packed, rim, wet_wide, previous, arrived, reply,
    load_sem, store_sem, send_sem, recv_sem, own_sem, row_send, row_recv, edge_send, edge_recv,
):
    ox, oy = lax.axis_index("ox"), lax.axis_index("oy")
    me = ox * 8 + oy
    loads = []
    for c in range(CHUNKS):
        at = pl.ds(c * CHUNK, CHUNK)
        loads.append(pltpu.make_async_copy(state_hbm.at[at], state.at[at], load_sem.at[c]))
        loads[-1].start()

    barrier = pltpu.get_barrier_semaphore()

    def partner(k):
        t = lax.rem(me + k, DEVICES)
        return t, (t // 8, lax.rem(t, 8))

    def greet(k, carry):
        pl.semaphore_signal(barrier, inc=1, device_id=partner(k)[1], device_id_type=MESH)
        return carry

    rim[...] = jnp.zeros_like(rim)
    previous[...] = jnp.zeros_like(previous)
    lax.fori_loop(1, DEVICES, greet, 0)
    pl.semaphore_wait(barrier, DEVICES - 1)

    def to_all(source, target, count, i):
        def send(k, carry):
            t, device = partner(k)
            pltpu.make_async_remote_copy(
                source.at[pl.ds(pl.multiple_of(t * PITCH, PITCH), count)],
                target.at[pl.ds(pl.multiple_of(me * PITCH, PITCH), count)],
                send_sem.at[i], recv_sem.at[i], device_id=device, device_id_type=MESH,
            ).start()
            return carry

        lax.fori_loop(1, DEVICES, send, 0)
        mine = pl.ds(pl.multiple_of(me * PITCH, PITCH), count)
        own = pltpu.make_async_copy(source.at[mine], target.at[mine], own_sem.at[i])
        own.start()
        return own

    def finish(source, target, count, i, own):
        rows = pl.ds(0, (DEVICES - 1) * count)
        pltpu.make_async_copy(source.at[rows], target.at[rows], send_sem.at[i]).wait()
        pltpu.make_async_copy(source.at[rows], target.at[rows], recv_sem.at[i]).wait()
        own.wait()

    own = to_all(out_hbm, arrived, SENT, 0)

    up, down = lax.rem(ox + 15, 16), lax.rem(ox + 1, 16)
    back, ahead = lax.rem(oy + 7, 8), lax.rem(oy + 1, 8)
    row_copies = []
    for c in range(CHUNKS):
        at = pl.ds(c * CHUNK, CHUNK)
        for d, (mine, there, device) in enumerate(((14, 6, down), (0, 0, up))):
            copy = pltpu.make_async_remote_copy(
                state_hbm.at[at, pl.ds(mine, 2)], rims.at[at, pl.ds(there, 2)],
                row_send.at[c, d], row_recv.at[c, d], device_id=(device, oy), device_id_type=MESH,
            )
            copy.start()
            row_copies.append(copy)
    edge_copies = []

    def edge(source, target, device):
        n = len(edge_copies)
        copy = pltpu.make_async_remote_copy(
            source, target, edge_send.at[n], edge_recv.at[n], device_id=device, device_id_type=MESH
        )
        copy.start()
        edge_copies.append(copy)

    edge(mask_ref.at[pl.ds(8, 8)], mask_rims.at[0], (down, oy))
    edge(mask_ref.at[pl.ds(0, 8)], mask_rims.at[1], (up, oy))

    for load in loads:
        load.wait()
    pack_columns(state, mask_ref, packed)
    for side, y in ((0, back), (1, ahead)):
        edge(packed.at[side], rim.at[side, :, pl.ds(0, ROWS)], (ox, y))
        edge(packed.at[side, :, pl.ds(0, 1)], rim.at[side, :, pl.ds(16, 1)], (up, y))
        edge(packed.at[side, :, pl.ds(15, 1)], rim.at[side, :, pl.ds(23, 1)], (down, y))

    sweep_up(state, mask_ref, depth_ref, scale_ref, value, ratio, response.at[0])

    for copy in edge_copies:
        copy.wait()
    wet = mask_ref[...].astype(F32)
    row8 = iota((8, COLS), 0)
    below = mask_rims[1].astype(F32) * (ox < 15).astype(F32)
    above = mask_rims[0].astype(F32) * (ox > 0).astype(F32)
    tall = jnp.concatenate([wet, jnp.where(row8 < 4, below, above)], axis=0)
    side = side_columns(rim, SLABS)
    lane = iota((24, 128), 1)
    row = iota((24, 128), 0)
    ok = jnp.where(lane < 64, (oy < 7).astype(F32), (oy > 0).astype(F32))
    ok = ok * jnp.where(row < 16, 1.0, jnp.where(row < 20, (ox < 15).astype(F32), (ox > 0).astype(F32)))
    wet_wide[...] = jnp.concatenate([tall, side * ok], axis=1)
    for copy in row_copies[:2]:
        copy.wait()
    level = functools.partial(
        ocean_level, state=state, rims=rims, rim=rim, wet_wide=wet_wide, value=value, ratio=ratio,
        response=response, previous=previous,
    )
    level(jnp.int32(0))

    finish(out_hbm, arrived, SENT, 0, own)
    ids = arrived[pl.ds(STRIPS, 128, stride=PITCH), :]
    ids = jnp.concatenate([ids[:, 0:1], ids[:, 1:2]], axis=0)
    lane = iota((256, 128), 1)
    hit = (ids == (lane & 15).astype(F32)) & (lane < 48)
    spread = hit.astype(F32)
    gather = spread.T[:ROWS].astype(BF16)
    spread = spread.astype(BF16)
    for f in range(FIELDS):
        for h in range(2):
            lanes = pl.ds(128 * h, 128)
            strip = 2 * f + h
            got = jnp.concatenate(
                [arrived[pl.ds(j * 12 + strip, 128, stride=PITCH), :] for j in range(2)], axis=0
            )
            hi, lo = split2(got)
            flux = jnp.dot(gather, hi, preferred_element_type=F32) + jnp.dot(gather, lo, preferred_element_type=F32)
            forcing = FORCING * mask_ref[:, lanes].astype(F32) * flux
            forced[f, :, lanes] = forcing
            surface = value[f, :, lanes] + response[0, :, lanes] * forcing
            top = surface.astype(BF16)
            rest = surface - top.astype(F32)
            middle = rest.astype(BF16)
            last = (rest - middle.astype(F32)).astype(BF16)
            right = jnp.concatenate([top, middle, last, jnp.zeros((80, 128), BF16)], axis=0)
            back_rows = jnp.dot(spread, right, preferred_element_type=F32)
            for j in range(2):
                reply[pl.ds(j * 12 + strip, 128, stride=PITCH), :] = back_rows[j * 128:(j + 1) * 128]
    own = to_all(reply, answered, STRIPS, 1)

    stores = []
    for c in range(CHUNKS):
        if c > 0:
            for copy in row_copies[2 * c:2 * c + 2]:
                copy.wait()

        def step(k, carry):
            level(k)
            return carry

        lax.fori_loop(max(1, c * CHUNK_LEVELS), (c + 1) * CHUNK_LEVELS, step, 0)
        at = pl.ds(c * CHUNK, CHUNK)
        stores.append(pltpu.make_async_copy(value.at[at], base_hbm.at[at], store_sem.at[c]))
        stores[-1].start()
    finish(reply, answered, STRIPS, 1, own)
    for store in stores:
        store.wait()


def exchange_call(outgoing, state, mask, depth, scale):
    vmem = pl.BlockSpec(memory_space=pltpu.VMEM)
    anywhere = pl.BlockSpec(memory_space=pl.ANY)
    dma = pltpu.SemaphoreType.DMA
    return pl.pallas_call(
        exchange_kernel,
        out_shape=(
            jax.ShapeDtypeStruct((SLABS, ROWS, COLS), F32),
            jax.ShapeDtypeStruct((LEVELS, ROWS, COLS), F32),
            jax.ShapeDtypeStruct((FIELDS, ROWS, COLS), F32),
            jax.ShapeDtypeStruct((DEVICES * PITCH, 128), F32),
        ),
        in_specs=[anywhere, anywhere, vmem, vmem, vmem],
        out_specs=(anywhere, vmem, vmem, vmem),
        scratch_shapes=[
            pltpu.VMEM((SLABS, ROWS, COLS), F32),
            pltpu.VMEM((SLABS, ROWS, COLS), F32),
            pltpu.VMEM((LEVELS, ROWS, COLS), F32),
            pltpu.VMEM((SLABS, 8, COLS), F32),
            pltpu.VMEM((2, 8, COLS), jnp.int32),
            pltpu.VMEM((2, GROUPS, ROWS, 128), F32),
            pltpu.VMEM((2, GROUPS, 24, 128), F32),
            pltpu.VMEM((24, 384), F32),
            pltpu.VMEM((FIELDS, ROWS, COLS), F32),
            pltpu.VMEM((DEVICES * PITCH, 128), F32),
            pltpu.VMEM((DEVICES * PITCH, 128), F32),
            dma((CHUNKS,)), dma((CHUNKS,)), dma((2,)), dma((2,)), dma((2,)),
            dma((CHUNKS, 2)), dma((CHUNKS, 2)), dma((8,)), dma((8,)),
        ],
        compiler_params=pltpu.CompilerParams(
            collective_id=0, has_side_effects=True, vmem_limit_bytes=50 << 20
        ),
        name="exchange",
    )(outgoing, state, mask, depth, scale)


LAST_STEPS = 16
LAST_PAIRS = PAIRS // LAST_STEPS
LAST_LEVELS = LEVELS // LAST_STEPS


def last_kernel(src_ref, weight_ref, base_ref, response_ref, forced_ref, answered_ref, dest_ref,
                ocean_ref, surface_ref, rows, total):
    step = pl.program_id(0)

    @pl.when(step == 0)
    def _():
        total[...] = jnp.zeros_like(total)
        rows[...] = jnp.zeros_like(rows)
        down, across = column_square(dest_ref)
        same = (down == across) & (iota((128, 128), 1) < iota((128, 128), 0))
        rank = jnp.sum(same.astype(F32), axis=1, keepdims=True)
        dest_here = down == iota((128, 128), 1).astype(F32)
        pick = jnp.concatenate(
            [(dest_here & (rank == float(j))).astype(F32).astype(BF16) for j in range(2)], axis=1
        )
        for f in range(FIELDS):
            for h in range(2):
                got = jnp.concatenate(
                    [answered_ref[pl.ds(j * 12 + 2 * f + h, 128, stride=PITCH), :] for j in range(2)], axis=0
                )
                hi, lo = split2(got)
                rows[pl.ds(h * 1024 + f, 128, stride=8), :] = (
                    jnp.dot(pick, hi, preferred_element_type=F32) + jnp.dot(pick, lo, preferred_element_type=F32)
                )

    for k in range(LAST_LEVELS):
        for f in range(FIELDS):
            ocean_ref[k * FIELDS + f] = base_ref[k * FIELDS + f] + response_ref[k] * forced_ref[f]

    for i in range(LAST_PAIRS):
        g = step * LAST_PAIRS + i
        row = jnp.concatenate(
            [rows[pl.ds(pl.multiple_of(h * 1024 + g * 8, 8), 8), :] for h in range(2)], axis=1
        )
        hi = row.astype(BF16).astype(F32)
        left = jnp.concatenate([hi, row - hi], axis=0).astype(BF16)
        top, low = split2(weight_ref[i])
        right = jnp.concatenate([top, low], axis=0)
        both = lax.dot_general(left, right, (((1,), (1,)), ((), ())), preferred_element_type=F32)
        both = both[:8] + both[8:]
        at = src_ref[g]
        total[at] = total[at] + both[:, :128] + both[:, 128:]

    @pl.when(step == LAST_STEPS - 1)
    def _():
        surface_ref[...] = total[:, :FIELDS, :]


def last_call(pair_weight, base, response, forced, answered, pair_src, pair_dest):
    whole = lambda shape: pl.BlockSpec(shape, lambda i, s: (0,) * len(shape))
    part = LAST_LEVELS * FIELDS
    return pl.pallas_call(
        last_kernel,
        out_shape=(
            jax.ShapeDtypeStruct((SLABS, ROWS, COLS), F32),
            jax.ShapeDtypeStruct((BLOCKS, FIELDS, 128), F32),
        ),
        grid_spec=pltpu.PrefetchScalarGridSpec(
            num_scalar_prefetch=1,
            grid=(LAST_STEPS,),
            in_specs=[
                pl.BlockSpec((LAST_PAIRS, 128, COLS), lambda i, s: (i, 0, 0)),
                pl.BlockSpec((part, ROWS, COLS), lambda i, s: (i, 0, 0)),
                pl.BlockSpec((LAST_LEVELS, ROWS, COLS), lambda i, s: (i, 0, 0)),
                whole((FIELDS, ROWS, COLS)),
                whole((DEVICES * PITCH, 128)),
                whole((PAIRS, 1)),
            ],
            out_specs=(
                pl.BlockSpec((part, ROWS, COLS), lambda i, s: (i, 0, 0)),
                whole((BLOCKS, FIELDS, 128)),
            ),
            scratch_shapes=[
                pltpu.VMEM((2048, 128), F32),
                pltpu.VMEM((BLOCKS, 8, 128), F32),
            ],
        ),
        compiler_params=pltpu.CompilerParams(vmem_limit_bytes=40 << 20),
        name="outputs",
    )(pair_src, pair_weight, base, response, forced, answered, pair_dest)


def shards(atm_flux, pair_weight, pair_src, pair_dest, pair_block, ocean_state, land_mask, kpp_depth, mixing_scale):
    outgoing = flux_call(pair_weight, atm_flux, pair_src, pair_dest, pair_block)
    state = ocean_state.reshape(SLABS, ROWS, COLS)
    base, response, forced, answered = exchange_call(outgoing, state, land_mask, kpp_depth, mixing_scale)
    ocean, surface = last_call(pair_weight, base, response, forced, answered, pair_src, pair_dest)
    return ocean.reshape(LEVELS, FIELDS, ROWS, COLS), surface


def solution(mesh):
    return jax.shard_map(
        shards,
        mesh=mesh,
        in_specs=(
            P(("ox", "oy"), None, None),
            P(("ox", "oy"), None, None),
            P(("ox", "oy")),
            P(("ox", "oy"), None),
            P(("ox", "oy")),
            P(None, None, "ox", "oy"),
            P("ox", "oy"),
            P("ox", "oy"),
            P("ox", "oy"),
        ),
        out_specs=(P(None, None, "ox", "oy"), P(("ox", "oy"), None, None)),
        check_vma=False,
    )
```

```python
import functools

import jax
import jax.numpy as jnp
from jax import lax
from jax.experimental import pallas as pl
from jax.experimental.pallas import tpu as pltpu
from jax.sharding import PartitionSpec as P

MESH = pl.DeviceIdType.MESH
F32 = jnp.float32
BF16 = jnp.bfloat16
VISCOSITY = 0.025
FORCING = 0.5
BACKGROUND = 0.05

DEVICES = 128
FIELDS = 6
LEVELS = 80
SLABS = LEVELS * FIELDS
ROWS = 16
COLS = 256
PAIRS = 96
BLOCKS = 32
STRIPS = 24
PITCH = 32
SENT = 25
GROUP = 64
GROUPS = 8
CHUNKS = 5
EARLY = 2
BATCH = 4
LIMIT_R = 54
LIMIT_L = 58
CHUNK_LEVELS = LEVELS // CHUNKS
CHUNK = SLABS // CHUNKS


def split2(v):
    hi = v.astype(BF16)
    lo = (v - hi.astype(F32)).astype(BF16)
    return hi, lo


def iota(shape, dim):
    return lax.broadcasted_iota(jnp.int32, shape, dim)


def row_square(dest_ref):
    row = jnp.concatenate([dest_ref[...], jnp.full((1, 128 - PAIRS), -1, jnp.int32)], axis=1)
    across = jnp.broadcast_to(row.astype(F32), (128, 128))
    return across.T, across


FLUX_STEP = 8


def part_copy(weight_hbm, weights, sem, i, count):
    at = pl.ds(i * count, count)
    return pltpu.make_async_copy(weight_hbm.at[at], weights.at[at], sem.at[i])


def flux_kernel(src_ref, weight_hbm, flux_ref, dest_ref, block_ref, out_ref, parts, contrib, weights, sem):
    step = pl.program_id(0)

    @pl.when(step == 0)
    def _():
        for i in range(PAIRS // FLUX_STEP):
            part_copy(weight_hbm, weights, sem, i, FLUX_STEP).start()
        contrib[...] = jnp.zeros_like(contrib)

        def prepare(b, carry):
            rows = jnp.concatenate([flux_ref[:, b, :], jnp.zeros((2, 128), F32)], axis=0)
            hi = rows.astype(BF16).astype(F32)
            both = jnp.concatenate([hi, rows - hi], axis=0).astype(BF16)
            parts[b] = jnp.concatenate([both, both], axis=1)
            return carry

        lax.fori_loop(0, BLOCKS, prepare, 0)

    part_copy(weight_hbm, weights, sem, step, FLUX_STEP).wait()
    for i in range(FLUX_STEP):
        g = step * FLUX_STEP + i
        left = parts[src_ref[g]]
        hi, lo = split2(weights[g])
        right = jnp.concatenate([hi, lo], axis=0)
        both = jnp.dot(left, right, preferred_element_type=F32)
        value = both[:8] + both[8:]
        at = pl.multiple_of(g * 8, 8)
        contrib[pl.ds(at, 8), :] = value[:, :128]
        contrib[pl.ds(pl.multiple_of(1024 + g * 8, 8), 8), :] = value[:, 128:]

    @pl.when(step == pl.num_programs(0) - 1)
    def _():
        down, across = row_square(dest_ref)
        same = (down == across) & (iota((128, 128), 0) < iota((128, 128), 1))
        rank = jnp.sum(same.astype(F32), axis=0, keepdims=True)
        dest_here = across == iota((128, 128), 0).astype(F32)
        places = [dest_here & (rank == float(j)) for j in range(2)]
        rows = jnp.concatenate([block_ref[...].astype(F32), jnp.zeros((1, 128 - PAIRS), F32)], axis=1) + 1.0
        ids = [jnp.sum(jnp.where(p, rows, 0.0), axis=1, keepdims=True) - 1.0 for p in places]
        lane = iota((128, 128), 1)
        out_ref[pl.ds(STRIPS, 128, stride=PITCH), :] = jnp.where(lane == 0, ids[0], ids[1])
        place = jnp.concatenate([p.astype(F32).astype(BF16) for p in places], axis=0)
        place = jnp.concatenate([place, place], axis=1)
        for f in range(FIELDS):
            for h in range(2):
                hi, lo = split2(contrib[pl.ds(h * 1024 + f, 128, stride=8), :])
                got = jnp.dot(place, jnp.concatenate([hi, lo], axis=0), preferred_element_type=F32)
                for j in range(2):
                    out_ref[pl.ds(j * 12 + 2 * f + h, 128, stride=PITCH), :] = got[j * 128:(j + 1) * 128]


def flux_call(pair_weight, atm_flux, pair_src, pair_dest, pair_block):
    whole = lambda shape: pl.BlockSpec(shape, lambda i, s: (0,) * len(shape))
    return pl.pallas_call(
        flux_kernel,
        out_shape=jax.ShapeDtypeStruct((DEVICES * PITCH, 128), F32),
        grid_spec=pltpu.PrefetchScalarGridSpec(
            num_scalar_prefetch=1,
            grid=(PAIRS // FLUX_STEP,),
            in_specs=[
                pl.BlockSpec(memory_space=pl.ANY),
                whole((FIELDS, BLOCKS, 128)),
                whole((1, PAIRS)),
                whole((1, PAIRS)),
            ],
            out_specs=whole((DEVICES * PITCH, 128)),
            scratch_shapes=[
                pltpu.VMEM((BLOCKS, 16, 256), BF16),
                pltpu.VMEM((2048, 128), F32),
                pltpu.VMEM((PAIRS, 128, COLS), F32),
                pltpu.SemaphoreType.DMA((PAIRS // FLUX_STEP,)),
            ],
        ),
        compiler_params=pltpu.CompilerParams(vmem_limit_bytes=56 << 20),
        name="contributions",
    )(pair_src, pair_weight, jnp.transpose(atm_flux, (1, 0, 2)), pair_dest.reshape(1, PAIRS), pair_block.reshape(1, PAIRS))


def pack_columns(state, mask_ref, packed):
    lane = iota((ROWS, 128), 1)

    def group(g, carry):
        first = jnp.zeros((ROWS, 128), F32)
        last = jnp.zeros((ROWS, 128), F32)
        for j in range(GROUP):
            slab = jnp.minimum(g * GROUP + j, SLABS - 1)
            both = jnp.where(lane < 64, state[slab, :, :128], state[slab, :, 128:])
            if j:
                both = pltpu.roll(both, 2 * j, 1)
            first = jnp.where(lane >= 2 * j, both, first)
            if j == 0:
                last = both
            else:
                last = jnp.where((lane >= 2 * j - 2) & (lane < 126), both, last)
        packed[0, g] = first
        packed[1, g] = pltpu.roll(last, 2, 1)
        return carry

    lax.fori_loop(0, GROUPS, group, 0)
    wet = mask_ref[...].astype(F32)
    g, shift = SLABS // GROUP, 2 * (SLABS % GROUP)
    here = (lane == shift) | (lane == shift + 1)
    packed[0, g] = jnp.where(here, pltpu.roll(wet[:, :128], shift, 1), packed[0, g])
    packed[1, g] = jnp.where(here, pltpu.roll(wet[:, 128:], shift + 2, 1), packed[1, g])


def side_setup(packed, rim, side_mask, side_state, side_first):
    at, here = SLABS // GROUP, 2 * (SLABS % GROUP)

    def wet_of(block):
        rows = block.shape[0]
        even = (iota((rows, 128), 1) & 1) == 0
        return jnp.where(even, block[:, here:here + 1], block[:, here + 1:here + 2])

    wets = [wet_of(rim[s, at]) * side_mask[s] for s in range(2)]
    owns = [wet_of(packed[s, at]) for s in range(2)]
    even = (iota((24, 128), 1) & 1) == 0

    def group(g, carry):
        right, left = wets[0] * rim[0, g], wets[1] * rim[1, g]
        side_state[g] = jnp.where(even, right, left)
        own_low, own_high = owns[0] * packed[0, g], owns[1] * packed[1, g]
        tall = lambda v: (pltpu.roll(v, 23, 0) + pltpu.roll(v, 1, 0) - 4.0 * v)[:ROWS]
        first_right = wets[0][:ROWS] * (tall(right) + pltpu.roll(right[:ROWS] + own_high, 127, 1))
        first_left = wets[1][:ROWS] * (tall(left) + pltpu.roll(left[:ROWS] + own_low, 1, 1))
        side_first[g] = jnp.where(even[:ROWS], first_right, first_left)
        return carry

    lax.fori_loop(0, GROUPS, group, 0)


def split_rows(parts):
    whole = jnp.concatenate(parts, axis=0)
    rest = whole - whole.astype(BF16).astype(F32)
    return jnp.concatenate([whole, rest], axis=0).astype(BF16)


def coupling_at(k, depth, scale):
    kf = k.astype(F32)
    sigma = (kf + 1.0) / depth
    rest = 1.0 - sigma
    profile = BACKGROUND + 6.75 * sigma * rest * rest
    value = scale * jnp.where(kf < depth, profile, BACKGROUND)
    return jnp.where(k >= 0, value, 0.0)


def sweep_up(state, mask_ref, depth_ref, scale_ref, value, ratio, first_inverse):
    for half in range(2):
        rows = pl.ds(8 * half, 8)
        wet = mask_ref[rows, :].astype(F32)
        depth = depth_ref[rows, :].astype(F32)
        scale = scale_ref[rows, :]

        def level(i, carry):
            below, open_now, values = carry
            k = LEVELS - 1 - i
            above = coupling_at(k - 1, depth, scale)
            inverse = 1.0 / (1.0 + above + below * open_now)
            ratio_now = above * inverse
            ratio[k, rows, :] = ratio_now
            weight = below * inverse
            wet_inverse = wet * inverse
            new = []
            for f in range(FIELDS):
                now = wet_inverse * state[k * FIELDS + f, rows, :] + weight * values[f]
                value[k * FIELDS + f, rows, :] = now
                new.append(now)

            @pl.when(k == 0)
            def _():
                first_inverse[rows, :] = inverse

            return above, 1.0 - ratio_now, tuple(new)

        zero = jnp.zeros((8, COLS), F32)
        lax.fori_loop(0, LEVELS, level, (zero, zero, (zero,) * FIELDS))


def ocean_levels(k, state, rims, side_state, side_first, wet_tall, along, value, ratio, response, previous):
    wet = wet_tall[...]
    count = BATCH * FIELDS
    start = k * FIELDS

    def sides(source, slab, rows):
        g = slab // GROUP
        values = pltpu.roll(source[g], 127 - 2 * (slab - g * GROUP), 1)
        lane = iota((rows, 128), 1)
        return jnp.concatenate([jnp.where(lane == 0, values, 0.0), jnp.where(lane == 127, values, 0.0)], axis=1)

    masked = [wet * jnp.concatenate([state[start + i], rims[start + i]], axis=0) for i in range(count)]
    cross = jnp.dot(split_rows(masked), along[...], preferred_element_type=F32)
    firsts = []
    for i in range(count):
        v = masked[i]
        straight = cross[24 * i:24 * i + 24] + cross[24 * (count + i):24 * (count + i) + 24]
        total = (pltpu.roll(v, 23, 0) + pltpu.roll(v, 1, 0)) + (straight + sides(side_state, start + i, 24))
        firsts.append(wet * total)
    cross = jnp.dot(split_rows([v[:ROWS] for v in firsts]), along[...], preferred_element_type=F32)
    for level in range(BATCH):
        ratio_now = ratio[k + level]
        response[k + level] = jnp.where(
            k + level == 0, response[k + level], ratio_now * response[jnp.maximum(k + level - 1, 0)]
        )
        for f in range(FIELDS):
            i = level * FIELDS + f
            v = firsts[i]
            straight = cross[16 * i:16 * i + 16] + cross[16 * (count + i):16 * (count + i) + 16]
            total = (pltpu.roll(v, 23, 0) + pltpu.roll(v, 1, 0))[:ROWS] + (
                straight + sides(side_first, start + i, ROWS)
            )
            mixed = value[start + i] + ratio_now * previous[f]
            previous[f] = mixed
            value[start + i] = mixed - VISCOSITY * (wet[:ROWS] * total)


def exchange_kernel(
    out_hbm, state_hbm, mask_ref, depth_ref, scale_ref,
    base_hbm, response, forced, answered,
    state, value, ratio, rims, mask_rims, packed, rim, side_mask, side_state, side_first, wet_tall, along, previous,
    arrived, reply, load_sem, store_sem, send_sem, recv_sem, own_sem, row_send, row_recv, edge_send, edge_recv,
):
    ox, oy = lax.axis_index("ox"), lax.axis_index("oy")
    me = ox * 8 + oy
    loads = []
    for c in range(CHUNKS):
        at = pl.ds(c * CHUNK, CHUNK)
        loads.append(pltpu.make_async_copy(state_hbm.at[at], state.at[at], load_sem.at[c]))
        loads[-1].start()

    barrier = pltpu.get_barrier_semaphore()

    def partner(k):
        t = lax.rem(me + k, DEVICES)
        return t, (t // 8, lax.rem(t, 8))

    def greet(k, carry):
        pl.semaphore_signal(barrier, inc=1, device_id=partner(k)[1], device_id_type=MESH)
        return carry

    rim[...] = jnp.zeros_like(rim)
    previous[...] = jnp.zeros_like(previous)
    lax.fori_loop(1, DEVICES, greet, 0)
    pl.semaphore_wait(barrier, DEVICES - 1)

    def rows_of(device, count):
        return pl.ds(pl.multiple_of(device * PITCH, PITCH), count)

    def to_all(source, target, count, i):
        mine = rows_of(me, count)

        def send(k, carry):
            dx, dy, dz = lax.rem(k, 4), lax.rem(k + k // 4, 4), lax.rem(k + k // 16, 4)
            to_x = lax.rem(ox // 4 + dy, 4) * 4 + lax.rem(lax.rem(ox, 4) + dx, 4)
            to_z = lax.rem(oy // 2 + dz, 4) * 2

            def one(to_y):
                pltpu.make_async_remote_copy(
                    source.at[rows_of(to_x * 8 + to_y, count)], target.at[mine], send_sem.at[i], recv_sem.at[i],
                    device_id=(to_x, to_y), device_id_type=MESH,
                ).start()

            one(to_z + lax.rem(oy + 1, 2))

            @pl.when(k > 0)
            def _():
                one(to_z + lax.rem(oy, 2))

            return carry

        lax.fori_loop(0, DEVICES // 2, send, 0)
        own = pltpu.make_async_copy(source.at[mine], target.at[mine], own_sem.at[i])
        own.start()
        return own

    def finish(source, target, count, i, own):
        rows = pl.ds(0, (DEVICES - 1) * count)
        pltpu.make_async_copy(source.at[rows], target.at[rows], recv_sem.at[i]).wait()
        pltpu.make_async_copy(source.at[rows], target.at[rows], send_sem.at[i]).wait()
        own.wait()

    own = to_all(out_hbm, arrived, SENT, 0)

    up, down = lax.rem(ox + 15, 16), lax.rem(ox + 1, 16)
    back, ahead = lax.rem(oy + 7, 8), lax.rem(oy + 1, 8)
    row_copies = []
    for c in range(CHUNKS):
        at = pl.ds(c * CHUNK, CHUNK)
        for d, (mine, there, device) in enumerate(((14, 6, down), (0, 0, up))):
            copy = pltpu.make_async_remote_copy(
                state_hbm.at[at, pl.ds(mine, 2)], rims.at[at, pl.ds(there, 2)],
                row_send.at[c, d], row_recv.at[c, d], device_id=(device, oy), device_id_type=MESH,
            )
            copy.start()
            row_copies.append(copy)
    edge_copies = []

    def edge(source, target, device):
        n = len(edge_copies)
        copy = pltpu.make_async_remote_copy(
            source, target, edge_send.at[n], edge_recv.at[n], device_id=device, device_id_type=MESH
        )
        copy.start()
        edge_copies.append(copy)

    edge(mask_ref.at[pl.ds(8, 8)], mask_rims.at[0], (down, oy))
    edge(mask_ref.at[pl.ds(0, 8)], mask_rims.at[1], (up, oy))

    for load in loads:
        load.wait()
    pack_columns(state, mask_ref, packed)
    for side, near in ((0, back), (1, ahead)):
        edge(packed.at[side], rim.at[side, :, pl.ds(0, ROWS)], (ox, near))
        edge(packed.at[side, :, pl.ds(0, 1)], rim.at[side, :, pl.ds(16, 1)], (up, near))
        edge(packed.at[side, :, pl.ds(15, 1)], rim.at[side, :, pl.ds(23, 1)], (down, near))

    sweep_up(state, mask_ref, depth_ref, scale_ref, value, ratio, response.at[0])

    for copy in edge_copies:
        copy.wait()
    wet = mask_ref[...].astype(F32)
    row8 = iota((8, COLS), 0)
    below = mask_rims[1].astype(F32) * (ox < 15).astype(F32)
    above = mask_rims[0].astype(F32) * (ox > 0).astype(F32)
    wet_tall[...] = jnp.concatenate([wet, jnp.where(row8 < 4, below, above)], axis=0)
    row = iota((24, 128), 0)
    inside = jnp.where(row < 16, 1.0, jnp.where(row < 20, (ox < 15).astype(F32), (ox > 0).astype(F32)))
    side_mask[0] = inside * (oy < 7).astype(F32)
    side_mask[1] = inside * (oy > 0).astype(F32)
    side_setup(packed, rim, side_mask, side_state, side_first)
    apart = iota((COLS, COLS), 0) - iota((COLS, COLS), 1)
    along[...] = jnp.where(apart == 0, -4.0, jnp.where((apart == 1) | (apart == -1), 1.0, 0.0)).astype(BF16)
    level = functools.partial(
        ocean_levels, state=state, rims=rims, side_state=side_state, side_first=side_first, wet_tall=wet_tall,
        along=along, value=value, ratio=ratio, response=response, previous=previous,
    )

    stores = []

    def chunk_levels(c):
        for copy in row_copies[2 * c:2 * c + 2]:
            copy.wait()

        def step(i, carry):
            level(c * CHUNK_LEVELS + i * BATCH)
            return carry

        lax.fori_loop(0, CHUNK_LEVELS // BATCH, step, 0)
        at = pl.ds(c * CHUNK, CHUNK)
        stores.append(pltpu.make_async_copy(value.at[at], base_hbm.at[at], store_sem.at[c]))
        stores[-1].start()

    for c in range(EARLY):
        chunk_levels(c)

    finish(out_hbm, arrived, SENT, 0, own)
    ids = arrived[pl.ds(STRIPS, 128, stride=PITCH), :]
    ids = jnp.concatenate([ids[:, 0:1], ids[:, 1:2]], axis=0)
    lane = iota((256, 128), 1)
    hit = (ids == (lane & 15).astype(F32)) & (lane < 48)
    spread = hit.astype(F32)
    gather = spread.T[:ROWS].astype(BF16)
    spread = spread.astype(BF16)
    for f in range(FIELDS):
        for h in range(2):
            lanes = pl.ds(128 * h, 128)
            strip = 2 * f + h
            got = jnp.concatenate(
                [arrived[pl.ds(j * 12 + strip, 128, stride=PITCH), :] for j in range(2)], axis=0
            )
            hi, lo = split2(got)
            flux = jnp.dot(gather, hi, preferred_element_type=F32) + jnp.dot(gather, lo, preferred_element_type=F32)
            forcing = FORCING * mask_ref[:, lanes].astype(F32) * flux
            forced[f, :, lanes] = forcing
            surface = value[f, :, lanes] + response[0, :, lanes] * forcing
            top = surface.astype(BF16)
            rest = surface - top.astype(F32)
            middle = rest.astype(BF16)
            last = (rest - middle.astype(F32)).astype(BF16)
            right = jnp.concatenate([top, middle, last, jnp.zeros((80, 128), BF16)], axis=0)
            back_rows = jnp.dot(spread, right, preferred_element_type=F32)
            for j in range(2):
                reply[pl.ds(j * 12 + strip, 128, stride=PITCH), :] = back_rows[j * 128:(j + 1) * 128]
    own = to_all(reply, answered, STRIPS, 1)
    for c in range(EARLY, CHUNKS):
        chunk_levels(c)
    finish(reply, answered, STRIPS, 1, own)
    for store in stores:
        store.wait()


def exchange_call(outgoing, state, mask, depth, scale):
    vmem = pl.BlockSpec(memory_space=pltpu.VMEM)
    anywhere = pl.BlockSpec(memory_space=pl.ANY)
    dma = pltpu.SemaphoreType.DMA
    return pl.pallas_call(
        exchange_kernel,
        out_shape=(
            jax.ShapeDtypeStruct((SLABS, ROWS, COLS), F32),
            jax.ShapeDtypeStruct((LEVELS, ROWS, COLS), F32),
            jax.ShapeDtypeStruct((FIELDS, ROWS, COLS), F32),
            jax.ShapeDtypeStruct((DEVICES * PITCH, 128), F32),
        ),
        in_specs=[anywhere, anywhere, vmem, vmem, vmem],
        out_specs=(anywhere, vmem, vmem, vmem),
        scratch_shapes=[
            pltpu.VMEM((SLABS, ROWS, COLS), F32),
            pltpu.VMEM((SLABS, ROWS, COLS), F32),
            pltpu.VMEM((LEVELS, ROWS, COLS), F32),
            pltpu.VMEM((SLABS, 8, COLS), F32),
            pltpu.VMEM((2, 8, COLS), jnp.int32),
            pltpu.VMEM((2, GROUPS, ROWS, 128), F32),
            pltpu.VMEM((2, GROUPS, 24, 128), F32),
            pltpu.VMEM((2, 24, 128), F32),
            pltpu.VMEM((GROUPS, 24, 128), F32),
            pltpu.VMEM((GROUPS, ROWS, 128), F32),
            pltpu.VMEM((24, COLS), F32),
            pltpu.VMEM((COLS, COLS), BF16),
            pltpu.VMEM((FIELDS, ROWS, COLS), F32),
            pltpu.VMEM((DEVICES * PITCH, 128), F32),
            pltpu.VMEM((DEVICES * PITCH, 128), F32),
            dma((CHUNKS,)), dma((CHUNKS,)), dma((2,)), dma((2,)), dma((2,)),
            dma((CHUNKS, 2)), dma((CHUNKS, 2)), dma((8,)), dma((8,)),
        ],
        compiler_params=pltpu.CompilerParams(
            collective_id=0, has_side_effects=True, vmem_limit_bytes=LIMIT_R << 20
        ),
        name="exchange",
    )(outgoing, state, mask, depth, scale)


LAST_STEPS = 16
LAST_PAIRS = PAIRS // LAST_STEPS
LAST_LEVELS = LEVELS // LAST_STEPS


def last_kernel(src_ref, weight_hbm, base_hbm, response_ref, forced_ref, answered_ref, dest_ref,
                ocean_ref, surface_ref, rows, total, weights, base_ref, sem, base_sem):
    step = pl.program_id(0)

    @pl.when(step == 0)
    def _():
        for i in range(LAST_STEPS):
            part_copy(base_hbm, base_ref, base_sem, i, LAST_LEVELS * FIELDS).start()
            part_copy(weight_hbm, weights, sem, i, LAST_PAIRS).start()
        total[...] = jnp.zeros_like(total)
        rows[...] = jnp.zeros_like(rows)
        down, across = row_square(dest_ref)
        same = (down == across) & (iota((128, 128), 1) < iota((128, 128), 0))
        rank = jnp.sum(same.astype(F32), axis=1, keepdims=True)
        dest_here = down == iota((128, 128), 1).astype(F32)
        pick = jnp.concatenate(
            [(dest_here & (rank == float(j))).astype(F32).astype(BF16) for j in range(2)], axis=1
        )
        for f in range(FIELDS):
            for h in range(2):
                got = jnp.concatenate(
                    [answered_ref[pl.ds(j * 12 + 2 * f + h, 128, stride=PITCH), :] for j in range(2)], axis=0
                )
                hi, lo = split2(got)
                rows[pl.ds(h * 1024 + f, 128, stride=8), :] = (
                    jnp.dot(pick, hi, preferred_element_type=F32) + jnp.dot(pick, lo, preferred_element_type=F32)
                )

    part_copy(base_hbm, base_ref, base_sem, step, LAST_LEVELS * FIELDS).wait()
    for k in range(LAST_LEVELS):
        for f in range(FIELDS):
            slab = step * (LAST_LEVELS * FIELDS) + k * FIELDS + f
            ocean_ref[k * FIELDS + f] = base_ref[slab] + response_ref[step * LAST_LEVELS + k] * forced_ref[f]
    part_copy(weight_hbm, weights, sem, step, LAST_PAIRS).wait()

    for i in range(LAST_PAIRS):
        g = step * LAST_PAIRS + i
        row = jnp.concatenate(
            [rows[pl.ds(pl.multiple_of(h * 1024 + g * 8, 8), 8), :] for h in range(2)], axis=1
        )
        left = split_rows([row])
        right = jnp.concatenate(list(split2(weights[g])), axis=0)
        both = lax.dot_general(left, right, (((1,), (1,)), ((), ())), preferred_element_type=F32)
        both = both[:8] + both[8:]
        at = src_ref[g]
        total[at] = total[at] + both[:, :128] + both[:, 128:]

    @pl.when(step == LAST_STEPS - 1)
    def _():
        for f in range(FIELDS):
            surface_ref[f] = total[:, f, :]


def last_call(pair_weight, base, response, forced, answered, pair_src, pair_dest):
    whole = lambda shape: pl.BlockSpec(shape, lambda i, s: (0,) * len(shape))
    part = LAST_LEVELS * FIELDS
    vmem = pl.BlockSpec(memory_space=pltpu.VMEM)
    return pl.pallas_call(
        last_kernel,
        out_shape=(
            jax.ShapeDtypeStruct((SLABS, ROWS, COLS), F32),
            jax.ShapeDtypeStruct((FIELDS, BLOCKS, 128), F32),
        ),
        grid_spec=pltpu.PrefetchScalarGridSpec(
            num_scalar_prefetch=1,
            grid=(LAST_STEPS,),
            in_specs=[
                pl.BlockSpec(memory_space=pl.ANY),
                pl.BlockSpec(memory_space=pl.ANY),
                vmem,
                vmem,
                vmem,
                vmem,
            ],
            out_specs=(
                pl.BlockSpec((part, ROWS, COLS), lambda i, s: (i, 0, 0)),
                whole((FIELDS, BLOCKS, 128)),
            ),
            scratch_shapes=[
                pltpu.VMEM((2048, 128), F32),
                pltpu.VMEM((BLOCKS, 8, 128), F32),
                pltpu.VMEM((PAIRS, 128, COLS), F32),
                pltpu.VMEM((SLABS, ROWS, COLS), F32),
                pltpu.SemaphoreType.DMA((LAST_STEPS,)),
                pltpu.SemaphoreType.DMA((LAST_STEPS,)),
            ],
        ),
        compiler_params=pltpu.CompilerParams(vmem_limit_bytes=LIMIT_L << 20),
        name="outputs",
    )(pair_src, pair_weight, base, response, forced, answered, pair_dest.reshape(1, PAIRS))


def shards(atm_flux, pair_weight, pair_src, pair_dest, pair_block, ocean_state, land_mask, kpp_depth, mixing_scale):
    outgoing = flux_call(pair_weight, atm_flux, pair_src, pair_dest, pair_block)
    state = ocean_state.reshape(SLABS, ROWS, COLS)
    base, response, forced, answered = exchange_call(outgoing, state, land_mask, kpp_depth, mixing_scale)
    ocean, surface = last_call(pair_weight, base, response, forced, answered, pair_src, pair_dest)
    return ocean.reshape(LEVELS, FIELDS, ROWS, COLS), jnp.transpose(surface, (1, 0, 2))


def solution(mesh):
    return jax.shard_map(
        shards,
        mesh=mesh,
        in_specs=(
            P(("ox", "oy"), None, None),
            P(("ox", "oy"), None, None),
            P(("ox", "oy")),
            P(("ox", "oy"), None),
            P(("ox", "oy")),
            P(None, None, "ox", "oy"),
            P("ox", "oy"),
            P("ox", "oy"),
            P("ox", "oy"),
        ),
        out_specs=(P(None, None, "ox", "oy"), P(("ox", "oy"), None, None)),
        check_vma=False,
    )
```

```python
import functools

import jax
import jax.numpy as jnp
from jax import lax
from jax.experimental import pallas as pl
from jax.experimental.pallas import tpu as pltpu
from jax.sharding import PartitionSpec as P

MESH = pl.DeviceIdType.MESH
F32 = jnp.float32
BF16 = jnp.bfloat16
VISCOSITY = 0.025
FORCING = 0.5
BACKGROUND = 0.05

DEVICES = 128
FIELDS = 6
LEVELS = 80
SLABS = LEVELS * FIELDS
ROWS = 16
COLS = 256
PAIRS = 96
BLOCKS = 32
STRIPS = 24
PITCH = 32
SENT = 25
GROUP = 64
GROUPS = 8
CHUNKS = 5
BOUNDS = (0, 4, 24, 44, 64, 80)
EARLY = 1
BATCH = 4
LIMIT_R = 58
LIMIT_L = 58
CHUNK = SLABS // CHUNKS


def split2(v):
    hi = v.astype(BF16)
    lo = (v - hi.astype(F32)).astype(BF16)
    return hi, lo


def iota(shape, dim):
    return lax.broadcasted_iota(jnp.int32, shape, dim)


def row_square(dest_ref):
    row = jnp.concatenate([dest_ref[...], jnp.full((1, 128 - PAIRS), -1, jnp.int32)], axis=1)
    across = jnp.broadcast_to(row.astype(F32), (128, 128))
    return across.T, across


FLUX_STEP = 8


def part_copy(weight_hbm, weights, sem, i, count):
    at = pl.ds(i * count, count)
    return pltpu.make_async_copy(weight_hbm.at[at], weights.at[at], sem.at[i])


def contributions(src_ref, weight_hbm, flux_ref, dest_ref, block_ref, out_ref, parts, contrib, weights, sem):
    contrib[...] = jnp.zeros_like(contrib)

    def prepare(b, carry):
        rows = jnp.concatenate([flux_ref[:, b, :], jnp.zeros((2, 128), F32)], axis=0)
        hi = rows.astype(BF16).astype(F32)
        both = jnp.concatenate([hi, rows - hi], axis=0).astype(BF16)
        parts[b] = jnp.concatenate([both, both], axis=1)
        return carry

    lax.fori_loop(0, BLOCKS, prepare, 0)

    def some(step, carry):
        part_copy(weight_hbm, weights, sem, step, FLUX_STEP).wait()
        for i in range(FLUX_STEP):
            g = step * FLUX_STEP + i
            left = parts[src_ref[g]]
            hi, lo = split2(weights[g])
            right = jnp.concatenate([hi, lo], axis=0)
            both = jnp.dot(left, right, preferred_element_type=F32)
            value = both[:8] + both[8:]
            at = pl.multiple_of(g * 8, 8)
            contrib[pl.ds(at, 8), :] = value[:, :128]
            contrib[pl.ds(pl.multiple_of(1024 + g * 8, 8), 8), :] = value[:, 128:]
        return carry

    lax.fori_loop(0, PAIRS // FLUX_STEP, some, 0)

    down, across = row_square(dest_ref)
    same = (down == across) & (iota((128, 128), 0) < iota((128, 128), 1))
    rank = jnp.sum(same.astype(F32), axis=0, keepdims=True)
    dest_here = across == iota((128, 128), 0).astype(F32)
    places = [dest_here & (rank == float(j)) for j in range(2)]
    rows = jnp.concatenate([block_ref[...].astype(F32), jnp.zeros((1, 128 - PAIRS), F32)], axis=1) + 1.0
    ids = [jnp.sum(jnp.where(p, rows, 0.0), axis=1, keepdims=True) - 1.0 for p in places]
    lane = iota((128, 128), 1)
    out_ref[pl.ds(STRIPS, 128, stride=PITCH), :] = jnp.where(lane == 0, ids[0], ids[1])
    place = jnp.concatenate([p.astype(F32).astype(BF16) for p in places], axis=0)
    place = jnp.concatenate([place, place], axis=1)
    for f in range(FIELDS):
        for h in range(2):
            hi, lo = split2(contrib[pl.ds(h * 1024 + f, 128, stride=8), :])
            got = jnp.dot(place, jnp.concatenate([hi, lo], axis=0), preferred_element_type=F32)
            for j in range(2):
                out_ref[pl.ds(j * 12 + 2 * f + h, 128, stride=PITCH), :] = got[j * 128:(j + 1) * 128]


def pack_columns(state, mask_ref, packed):
    lane = iota((ROWS, 128), 1)

    def group(g, carry):
        first = jnp.zeros((ROWS, 128), F32)
        last = jnp.zeros((ROWS, 128), F32)
        for j in range(GROUP):
            slab = jnp.minimum(g * GROUP + j, SLABS - 1)
            both = jnp.where(lane < 64, state[slab, :, :128], state[slab, :, 128:])
            if j:
                both = pltpu.roll(both, 2 * j, 1)
            first = jnp.where(lane >= 2 * j, both, first)
            if j == 0:
                last = both
            else:
                last = jnp.where((lane >= 2 * j - 2) & (lane < 126), both, last)
        packed[0, g] = first
        packed[1, g] = pltpu.roll(last, 2, 1)
        return carry

    lax.fori_loop(0, GROUPS, group, 0)
    wet = mask_ref[...].astype(F32)
    g, shift = SLABS // GROUP, 2 * (SLABS % GROUP)
    here = (lane == shift) | (lane == shift + 1)
    packed[0, g] = jnp.where(here, pltpu.roll(wet[:, :128], shift, 1), packed[0, g])
    packed[1, g] = jnp.where(here, pltpu.roll(wet[:, 128:], shift + 2, 1), packed[1, g])


def side_setup(packed, rim, side_mask, side_state, side_first):
    at, here = SLABS // GROUP, 2 * (SLABS % GROUP)

    def wet_of(block):
        rows = block.shape[0]
        even = (iota((rows, 128), 1) & 1) == 0
        return jnp.where(even, block[:, here:here + 1], block[:, here + 1:here + 2])

    wets = [wet_of(rim[s, at]) * side_mask[s] for s in range(2)]
    owns = [wet_of(packed[s, at]) for s in range(2)]
    even = (iota((24, 128), 1) & 1) == 0

    def group(g, carry):
        right, left = wets[0] * rim[0, g], wets[1] * rim[1, g]
        side_state[g] = jnp.where(even, right, left)
        own_low, own_high = owns[0] * packed[0, g], owns[1] * packed[1, g]
        tall = lambda v: (pltpu.roll(v, 23, 0) + pltpu.roll(v, 1, 0) - 4.0 * v)[:ROWS]
        first_right = wets[0][:ROWS] * (tall(right) + pltpu.roll(right[:ROWS] + own_high, 127, 1))
        first_left = wets[1][:ROWS] * (tall(left) + pltpu.roll(left[:ROWS] + own_low, 1, 1))
        side_first[g] = jnp.where(even[:ROWS], first_right, first_left)
        return carry

    lax.fori_loop(0, GROUPS, group, 0)


def split_rows(parts):
    whole = jnp.concatenate(parts, axis=0)
    rest = whole - whole.astype(BF16).astype(F32)
    return jnp.concatenate([whole, rest], axis=0).astype(BF16)


def coupling_at(k, depth, scale):
    kf = k.astype(F32)
    sigma = (kf + 1.0) / depth
    rest = 1.0 - sigma
    profile = BACKGROUND + 6.75 * sigma * rest * rest
    value = scale * jnp.where(kf < depth, profile, BACKGROUND)
    return jnp.where(k >= 0, value, 0.0)


def sweep_up(state, mask_ref, depth_ref, scale_ref, value, ratio, first_inverse):
    for half in range(2):
        rows = pl.ds(8 * half, 8)
        wet = mask_ref[rows, :].astype(F32)
        depth = depth_ref[rows, :].astype(F32)
        scale = scale_ref[rows, :]

        def level(i, carry):
            below, open_now, values = carry
            k = LEVELS - 1 - i
            above = coupling_at(k - 1, depth, scale)
            inverse = 1.0 / (1.0 + above + below * open_now)
            ratio_now = above * inverse
            ratio[k, rows, :] = ratio_now
            weight = below * inverse
            wet_inverse = wet * inverse
            new = []
            for f in range(FIELDS):
                now = wet_inverse * state[k * FIELDS + f, rows, :] + weight * values[f]
                value[k * FIELDS + f, rows, :] = now
                new.append(now)

            @pl.when(k == 0)
            def _():
                first_inverse[rows, :] = inverse

            return above, 1.0 - ratio_now, tuple(new)

        zero = jnp.zeros((8, COLS), F32)
        lax.fori_loop(0, LEVELS, level, (zero, zero, (zero,) * FIELDS))


def ocean_levels(k, state, rims, side_state, side_first, wet_tall, along, value, ratio, response, previous):
    wet = wet_tall[...]
    count = BATCH * FIELDS
    start = k * FIELDS

    def sides(source, slab, rows):
        g = slab // GROUP
        values = pltpu.roll(source[g], 127 - 2 * (slab - g * GROUP), 1)
        lane = iota((rows, 128), 1)
        return jnp.concatenate([jnp.where(lane == 0, values, 0.0), jnp.where(lane == 127, values, 0.0)], axis=1)

    masked = [wet * jnp.concatenate([state[start + i], rims[start + i]], axis=0) for i in range(count)]
    cross = jnp.dot(split_rows(masked), along[...], preferred_element_type=F32)
    firsts = []
    for i in range(count):
        v = masked[i]
        straight = cross[24 * i:24 * i + 24] + cross[24 * (count + i):24 * (count + i) + 24]
        total = (pltpu.roll(v, 23, 0) + pltpu.roll(v, 1, 0)) + (straight + sides(side_state, start + i, 24))
        firsts.append(wet * total)
    cross = jnp.dot(split_rows([v[:ROWS] for v in firsts]), along[...], preferred_element_type=F32)
    for level in range(BATCH):
        ratio_now = ratio[k + level]
        response[k + level] = jnp.where(
            k + level == 0, response[k + level], ratio_now * response[jnp.maximum(k + level - 1, 0)]
        )
        for f in range(FIELDS):
            i = level * FIELDS + f
            v = firsts[i]
            straight = cross[16 * i:16 * i + 16] + cross[16 * (count + i):16 * (count + i) + 16]
            total = (pltpu.roll(v, 23, 0) + pltpu.roll(v, 1, 0))[:ROWS] + (
                straight + sides(side_first, start + i, ROWS)
            )
            mixed = value[start + i] + ratio_now * previous[f]
            previous[f] = mixed
            value[start + i] = mixed - VISCOSITY * (wet[:ROWS] * total)


def span(c):
    return pl.ds(BOUNDS[c] * FIELDS, (BOUNDS[c + 1] - BOUNDS[c]) * FIELDS)


def exchange_kernel(
    src_ref, weight_hbm, flux_ref, dest_ref, block_ref, state_hbm, mask_ref, depth_ref, scale_ref,
    base_hbm, response, forced, answered,
    out_ref, parts, contrib, weights, weight_sem,
    state, value, ratio, rims, mask_rims, packed, rim, side_mask, side_state, side_first, wet_tall, along, previous,
    arrived, reply, load_sem, store_sem, send_sem, recv_sem, own_sem, row_send, row_recv, edge_send, edge_recv,
):
    ox, oy = lax.axis_index("ox"), lax.axis_index("oy")
    me = ox * 8 + oy
    loads = []
    for c in range(CHUNKS):
        at = pl.ds(c * CHUNK, CHUNK)
        loads.append(pltpu.make_async_copy(state_hbm.at[at], state.at[at], load_sem.at[c]))
        loads[-1].start()

    for i in range(PAIRS // FLUX_STEP):
        part_copy(weight_hbm, weights, weight_sem, i, FLUX_STEP).start()
    barrier = pltpu.get_barrier_semaphore()

    def partner(k):
        t = lax.rem(me + k, DEVICES)
        return t, (t // 8, lax.rem(t, 8))

    def greet(k, carry):
        pl.semaphore_signal(barrier, inc=1, device_id=partner(k)[1], device_id_type=MESH)
        return carry

    rim[...] = jnp.zeros_like(rim)
    previous[...] = jnp.zeros_like(previous)
    lax.fori_loop(1, DEVICES, greet, 0)
    pl.semaphore_wait(barrier, DEVICES - 1)

    def rows_of(device, count):
        return pl.ds(pl.multiple_of(device * PITCH, PITCH), count)

    def to_all(source, target, count, i):
        mine = rows_of(me, count)

        def send(k, carry):
            dx, dy, dz = lax.rem(k, 4), lax.rem(k + k // 4, 4), lax.rem(k + k // 16, 4)
            to_x = lax.rem(ox // 4 + dy, 4) * 4 + lax.rem(lax.rem(ox, 4) + dx, 4)
            to_z = lax.rem(oy // 2 + dz, 4) * 2

            def one(to_y):
                pltpu.make_async_remote_copy(
                    source.at[rows_of(to_x * 8 + to_y, count)], target.at[mine], send_sem.at[i], recv_sem.at[i],
                    device_id=(to_x, to_y), device_id_type=MESH,
                ).start()

            one(to_z + lax.rem(oy + 1, 2))

            @pl.when(k > 0)
            def _():
                one(to_z + lax.rem(oy, 2))

            return carry

        lax.fori_loop(0, DEVICES // 2, send, 0)
        own = pltpu.make_async_copy(source.at[mine], target.at[mine], own_sem.at[i])
        own.start()
        return own

    def finish(source, target, count, i, own):
        rows = pl.ds(0, (DEVICES - 1) * count)
        pltpu.make_async_copy(source.at[rows], target.at[rows], recv_sem.at[i]).wait()
        pltpu.make_async_copy(source.at[rows], target.at[rows], send_sem.at[i]).wait()
        own.wait()


    up, down = lax.rem(ox + 15, 16), lax.rem(ox + 1, 16)
    back, ahead = lax.rem(oy + 7, 8), lax.rem(oy + 1, 8)
    row_copies = []
    for c in range(CHUNKS):
        at = span(c)
        for d, (mine, there, device) in enumerate(((14, 6, down), (0, 0, up))):
            copy = pltpu.make_async_remote_copy(
                state_hbm.at[at, pl.ds(mine, 2)], rims.at[at, pl.ds(there, 2)],
                row_send.at[c, d], row_recv.at[c, d], device_id=(device, oy), device_id_type=MESH,
            )
            copy.start()
            row_copies.append(copy)
    edge_copies = []

    def edge(source, target, device):
        n = len(edge_copies)
        copy = pltpu.make_async_remote_copy(
            source, target, edge_send.at[n], edge_recv.at[n], device_id=device, device_id_type=MESH
        )
        copy.start()
        edge_copies.append(copy)

    edge(mask_ref.at[pl.ds(8, 8)], mask_rims.at[0], (down, oy))
    edge(mask_ref.at[pl.ds(0, 8)], mask_rims.at[1], (up, oy))

    for load in loads:
        load.wait()
    pack_columns(state, mask_ref, packed)
    for side, near in ((0, back), (1, ahead)):
        edge(packed.at[side], rim.at[side, :, pl.ds(0, ROWS)], (ox, near))
        edge(packed.at[side, :, pl.ds(0, 1)], rim.at[side, :, pl.ds(16, 1)], (up, near))
        edge(packed.at[side, :, pl.ds(15, 1)], rim.at[side, :, pl.ds(23, 1)], (down, near))

    contributions(src_ref, weight_hbm, flux_ref, dest_ref, block_ref, out_ref, parts, contrib, weights, weight_sem)
    own = to_all(out_ref, arrived, SENT, 0)
    sweep_up(state, mask_ref, depth_ref, scale_ref, value, ratio, response.at[0])

    for copy in edge_copies:
        copy.wait()
    wet = mask_ref[...].astype(F32)
    row8 = iota((8, COLS), 0)
    below = mask_rims[1].astype(F32) * (ox < 15).astype(F32)
    above = mask_rims[0].astype(F32) * (ox > 0).astype(F32)
    wet_tall[...] = jnp.concatenate([wet, jnp.where(row8 < 4, below, above)], axis=0)
    row = iota((24, 128), 0)
    inside = jnp.where(row < 16, 1.0, jnp.where(row < 20, (ox < 15).astype(F32), (ox > 0).astype(F32)))
    side_mask[0] = inside * (oy < 7).astype(F32)
    side_mask[1] = inside * (oy > 0).astype(F32)
    side_setup(packed, rim, side_mask, side_state, side_first)
    apart = iota((COLS, COLS), 0) - iota((COLS, COLS), 1)
    along[...] = jnp.where(apart == 0, -4.0, jnp.where((apart == 1) | (apart == -1), 1.0, 0.0)).astype(BF16)
    level = functools.partial(
        ocean_levels, state=state, rims=rims, side_state=side_state, side_first=side_first, wet_tall=wet_tall,
        along=along, value=value, ratio=ratio, response=response, previous=previous,
    )

    stores = []

    def chunk_levels(c):
        for copy in row_copies[2 * c:2 * c + 2]:
            copy.wait()

        def step(i, carry):
            level(BOUNDS[c] + i * BATCH)
            return carry

        lax.fori_loop(0, (BOUNDS[c + 1] - BOUNDS[c]) // BATCH, step, 0)
        at = span(c)
        stores.append(pltpu.make_async_copy(value.at[at], base_hbm.at[at], store_sem.at[c]))
        stores[-1].start()

    for c in range(EARLY):
        chunk_levels(c)

    finish(out_ref, arrived, SENT, 0, own)
    ids = arrived[pl.ds(STRIPS, 128, stride=PITCH), :]
    ids = jnp.concatenate([ids[:, 0:1], ids[:, 1:2]], axis=0)
    lane = iota((256, 128), 1)
    hit = (ids == (lane & 15).astype(F32)) & (lane < 48)
    spread = hit.astype(F32)
    gather = spread.T[:ROWS].astype(BF16)
    spread = spread.astype(BF16)
    for f in range(FIELDS):
        for h in range(2):
            lanes = pl.ds(128 * h, 128)
            strip = 2 * f + h
            got = jnp.concatenate(
                [arrived[pl.ds(j * 12 + strip, 128, stride=PITCH), :] for j in range(2)], axis=0
            )
            hi, lo = split2(got)
            flux = jnp.dot(gather, hi, preferred_element_type=F32) + jnp.dot(gather, lo, preferred_element_type=F32)
            forcing = FORCING * mask_ref[:, lanes].astype(F32) * flux
            forced[f, :, lanes] = forcing
            surface = value[f, :, lanes] + response[0, :, lanes] * forcing
            top = surface.astype(BF16)
            rest = surface - top.astype(F32)
            middle = rest.astype(BF16)
            last = (rest - middle.astype(F32)).astype(BF16)
            right = jnp.concatenate([top, middle, last, jnp.zeros((80, 128), BF16)], axis=0)
            back_rows = jnp.dot(spread, right, preferred_element_type=F32)
            for j in range(2):
                reply[pl.ds(j * 12 + strip, 128, stride=PITCH), :] = back_rows[j * 128:(j + 1) * 128]
    own = to_all(reply, answered, STRIPS, 1)
    for c in range(EARLY, CHUNKS):
        chunk_levels(c)
    finish(reply, answered, STRIPS, 1, own)
    for store in stores:
        store.wait()


def exchange_call(pair_src, pair_weight, atm_flux, pair_dest, pair_block, state, mask, depth, scale):
    vmem = pl.BlockSpec(memory_space=pltpu.VMEM)
    anywhere = pl.BlockSpec(memory_space=pl.ANY)
    dma = pltpu.SemaphoreType.DMA
    return pl.pallas_call(
        exchange_kernel,
        out_shape=(
            jax.ShapeDtypeStruct((SLABS, ROWS, COLS), F32),
            jax.ShapeDtypeStruct((LEVELS, ROWS, COLS), F32),
            jax.ShapeDtypeStruct((FIELDS, ROWS, COLS), F32),
            jax.ShapeDtypeStruct((DEVICES * PITCH, 128), F32),
        ),
        in_specs=[pl.BlockSpec(memory_space=pltpu.SMEM), anywhere, vmem, vmem, vmem, anywhere, vmem, vmem, vmem],
        out_specs=(anywhere, vmem, vmem, vmem),
        scratch_shapes=[
            pltpu.VMEM((DEVICES * PITCH, 128), F32),
            pltpu.VMEM((BLOCKS, 16, 256), BF16),
            pltpu.VMEM((2048, 128), F32),
            pltpu.VMEM((PAIRS, 128, COLS), F32),
            dma((PAIRS // FLUX_STEP,)),
            pltpu.VMEM((SLABS, ROWS, COLS), F32),
            pltpu.VMEM((SLABS, ROWS, COLS), F32),
            pltpu.VMEM((LEVELS, ROWS, COLS), F32),
            pltpu.VMEM((SLABS, 8, COLS), F32),
            pltpu.VMEM((2, 8, COLS), jnp.int32),
            pltpu.VMEM((2, GROUPS, ROWS, 128), F32),
            pltpu.VMEM((2, GROUPS, 24, 128), F32),
            pltpu.VMEM((2, 24, 128), F32),
            pltpu.VMEM((GROUPS, 24, 128), F32),
            pltpu.VMEM((GROUPS, ROWS, 128), F32),
            pltpu.VMEM((24, COLS), F32),
            pltpu.VMEM((COLS, COLS), BF16),
            pltpu.VMEM((FIELDS, ROWS, COLS), F32),
            pltpu.VMEM((DEVICES * PITCH, 128), F32),
            pltpu.VMEM((DEVICES * PITCH, 128), F32),
            dma((CHUNKS,)), dma((CHUNKS,)), dma((2,)), dma((2,)), dma((2,)),
            dma((CHUNKS, 2)), dma((CHUNKS, 2)), dma((8,)), dma((8,)),
        ],
        compiler_params=pltpu.CompilerParams(
            collective_id=0, has_side_effects=True, vmem_limit_bytes=LIMIT_R << 20
        ),
        name="exchange",
    )(
        pair_src, pair_weight, jnp.transpose(atm_flux, (1, 0, 2)), pair_dest.reshape(1, PAIRS),
        pair_block.reshape(1, PAIRS), state, mask, depth, scale,
    )


LAST_STEPS = 16
LAST_PAIRS = PAIRS // LAST_STEPS
LAST_LEVELS = LEVELS // LAST_STEPS


def last_kernel(src_ref, weight_hbm, base_hbm, response_ref, forced_ref, answered_ref, dest_ref,
                ocean_ref, surface_ref, rows, total, weights, base_ref, sem, base_sem):
    step = pl.program_id(0)

    @pl.when(step == 0)
    def _():
        for i in range(LAST_STEPS):
            part_copy(base_hbm, base_ref, base_sem, i, LAST_LEVELS * FIELDS).start()
            part_copy(weight_hbm, weights, sem, i, LAST_PAIRS).start()
        total[...] = jnp.zeros_like(total)
        rows[...] = jnp.zeros_like(rows)
        down, across = row_square(dest_ref)
        same = (down == across) & (iota((128, 128), 1) < iota((128, 128), 0))
        rank = jnp.sum(same.astype(F32), axis=1, keepdims=True)
        dest_here = down == iota((128, 128), 1).astype(F32)
        pick = jnp.concatenate(
            [(dest_here & (rank == float(j))).astype(F32).astype(BF16) for j in range(2)], axis=1
        )
        for f in range(FIELDS):
            for h in range(2):
                got = jnp.concatenate(
                    [answered_ref[pl.ds(j * 12 + 2 * f + h, 128, stride=PITCH), :] for j in range(2)], axis=0
                )
                hi, lo = split2(got)
                rows[pl.ds(h * 1024 + f, 128, stride=8), :] = (
                    jnp.dot(pick, hi, preferred_element_type=F32) + jnp.dot(pick, lo, preferred_element_type=F32)
                )

    part_copy(base_hbm, base_ref, base_sem, step, LAST_LEVELS * FIELDS).wait()
    for k in range(LAST_LEVELS):
        for f in range(FIELDS):
            slab = step * (LAST_LEVELS * FIELDS) + k * FIELDS + f
            ocean_ref[k * FIELDS + f] = base_ref[slab] + response_ref[step * LAST_LEVELS + k] * forced_ref[f]
    part_copy(weight_hbm, weights, sem, step, LAST_PAIRS).wait()

    for i in range(LAST_PAIRS):
        g = step * LAST_PAIRS + i
        row = jnp.concatenate(
            [rows[pl.ds(pl.multiple_of(h * 1024 + g * 8, 8), 8), :] for h in range(2)], axis=1
        )
        left = split_rows([row])
        right = jnp.concatenate(list(split2(weights[g])), axis=0)
        both = lax.dot_general(left, right, (((1,), (1,)), ((), ())), preferred_element_type=F32)
        both = both[:8] + both[8:]
        at = src_ref[g]
        total[at] = total[at] + both[:, :128] + both[:, 128:]

    @pl.when(step == LAST_STEPS - 1)
    def _():
        for f in range(FIELDS):
            surface_ref[f] = total[:, f, :]


def last_call(pair_weight, base, response, forced, answered, pair_src, pair_dest):
    whole = lambda shape: pl.BlockSpec(shape, lambda i, s: (0,) * len(shape))
    part = LAST_LEVELS * FIELDS
    vmem = pl.BlockSpec(memory_space=pltpu.VMEM)
    return pl.pallas_call(
        last_kernel,
        out_shape=(
            jax.ShapeDtypeStruct((SLABS, ROWS, COLS), F32),
            jax.ShapeDtypeStruct((FIELDS, BLOCKS, 128), F32),
        ),
        grid_spec=pltpu.PrefetchScalarGridSpec(
            num_scalar_prefetch=1,
            grid=(LAST_STEPS,),
            in_specs=[
                pl.BlockSpec(memory_space=pl.ANY),
                pl.BlockSpec(memory_space=pl.ANY),
                vmem,
                vmem,
                vmem,
                vmem,
            ],
            out_specs=(
                pl.BlockSpec((part, ROWS, COLS), lambda i, s: (i, 0, 0)),
                whole((FIELDS, BLOCKS, 128)),
            ),
            scratch_shapes=[
                pltpu.VMEM((2048, 128), F32),
                pltpu.VMEM((BLOCKS, 8, 128), F32),
                pltpu.VMEM((PAIRS, 128, COLS), F32),
                pltpu.VMEM((SLABS, ROWS, COLS), F32),
                pltpu.SemaphoreType.DMA((LAST_STEPS,)),
                pltpu.SemaphoreType.DMA((LAST_STEPS,)),
            ],
        ),
        compiler_params=pltpu.CompilerParams(vmem_limit_bytes=LIMIT_L << 20),
        name="outputs",
    )(pair_src, pair_weight, base, response, forced, answered, pair_dest.reshape(1, PAIRS))


def shards(atm_flux, pair_weight, pair_src, pair_dest, pair_block, ocean_state, land_mask, kpp_depth, mixing_scale):
    state = ocean_state.reshape(SLABS, ROWS, COLS)
    base, response, forced, answered = exchange_call(
        pair_src, pair_weight, atm_flux, pair_dest, pair_block, state, land_mask, kpp_depth, mixing_scale
    )
    ocean, surface = last_call(pair_weight, base, response, forced, answered, pair_src, pair_dest)
    return ocean.reshape(LEVELS, FIELDS, ROWS, COLS), jnp.transpose(surface, (1, 0, 2))


def solution(mesh):
    return jax.shard_map(
        shards,
        mesh=mesh,
        in_specs=(
            P(("ox", "oy"), None, None),
            P(("ox", "oy"), None, None),
            P(("ox", "oy")),
            P(("ox", "oy"), None),
            P(("ox", "oy")),
            P(None, None, "ox", "oy"),
            P("ox", "oy"),
            P("ox", "oy"),
            P("ox", "oy"),
        ),
        out_specs=(P(None, None, "ox", "oy"), P(("ox", "oy"), None, None)),
        check_vma=False,
    )
```
